256 devices in a mesh: rows: 4 (over y_lo, core), racks: 8 (over z), pods: 8 (over x, y_hi).
Axes of the slice: x: 4, y: 4 (y_hi: 2, y_lo: 2; y = y_hi * 2 + y_lo), z: 8, core: 2. Of those that a mesh axis runs over, the one named last changes fastest.
Arguments:
- tensor: float32 [8, 16384, 4096], P('rows', 'racks', 'pods'), may hold values from -7372 to 7372, as said below
- factor_b: float32 [16384, 64], P(('racks', 'pods')), may hold values from 0 to 1
- factor_c: float32 [4096, 64], P(('pods', 'racks')), may hold values from 0 to 1
Outputs:
- factor_a: float32 [8, 64], P('rows')
The draws below stay inside these ranges and needn't reach their ends.
Inputs may be any that keep to these rules, and one draw needn't show every extreme that they name: `tensor`: entries of order one times 0.2 * sqrt(67108864).
All inputs are finite; a program needn't handle non-finite values.
Results may differ from the reference program's by a relative error of at most 0.00013.
Values sent between devices are 32-bit elements; how exact they have to be, the bound alone decides.
No kernel may reach another device: no remote copies, remote signals or barrier semaphores. Data moves between devices by JAX's collectives and lax.ppermute only.
A program may use at most 64 MiB of HBM per device.

```python
import jax
import jax.numpy as jnp
from jax import lax

R = 64
I = 8
J = 16384
K = 4096


def draw_tensor(key, part):
    key = jax.random.fold_in(key, 11)
    bound = float((J * K) ** 0.5 * 9 // 10)
    base = jax.random.normal(key, (I, J, K), jnp.float32)
    return jnp.clip(base * (bound / 4.5), -bound, bound)


def shard_levels(rng, extent, shards, low, largest):
    factor_of = 1.0
    for dim, parts in shards:
        draws = jax.random.uniform(jax.random.fold_in(jax.random.fold_in(rng, 6), dim), (parts,), jnp.float32, low / len(shards), largest / len(shards))
        factor_of = factor_of * jnp.repeat(jnp.exp(draws), extent[dim] // parts).reshape((-1,) + (1,) * (len(extent) - 1 - dim))
    return factor_of


def setup_inputs(seed: int = 0) -> dict:
    keys = jax.random.split(jax.random.key(seed), 4)
    return {
        "tensor": draw_tensor(jax.random.fold_in(keys[3], 71), 0),
        "factor_b": jnp.clip(1.0 * jax.random.uniform(keys[1], (J, R), jnp.float32) ** shard_levels(keys[1], (J, R), ((0, 64),), -0.2, 0.2), 0.0, 1.0),
        "factor_c": jnp.clip(1.0 * jax.random.uniform(keys[2], (K, R), jnp.float32) ** shard_levels(keys[2], (K, R), ((0, 64),), -0.2, 0.2), 0.0, 1.0),
    }


def reference(tensor, factor_b, factor_c):
    highest = lax.Precision.HIGHEST
    gram_b = jnp.dot(factor_b.T.astype(jnp.float32), factor_b.astype(jnp.float32), precision=highest, preferred_element_type=jnp.float32)
    gram_c = jnp.dot(factor_c.T.astype(jnp.float32), factor_c.astype(jnp.float32), precision=highest, preferred_element_type=jnp.float32)
    normal_matrix = gram_b * gram_c

    def one_row(slab):
        mixed = jnp.dot(slab.astype(jnp.float32), factor_c.astype(jnp.float32), precision=highest, preferred_element_type=jnp.float32)
        return jnp.sum(mixed * factor_b, axis=0)
    mttkrp = lax.map(one_row, tensor)
    lower = jnp.linalg.cholesky(normal_matrix)
    return jax.scipy.linalg.cho_solve((lower, True), mttkrp.T).T
```

```python
import jax
import jax.numpy as jnp
from jax import lax
from jax.sharding import PartitionSpec as P

HIGHEST = lax.Precision.HIGHEST


def share(block, axes, n):
    return lax.all_to_all(jnp.broadcast_to(block[None], (n, *block.shape)), axes, 0, 0, tiled=True)


def body(tensor, factor_b, factor_c):
    racks, pods = lax.axis_size("racks"), lax.axis_size("pods")
    rank = factor_b.shape[1]
    gram_b_own = jnp.dot(factor_b.T, factor_b, precision=HIGHEST)
    first = share(jnp.concatenate([factor_c, gram_b_own], axis=1), "racks", racks)
    c_block = first[:, :, :rank].reshape(-1, rank)
    gram_b_pod = jnp.sum(first[:, :, rank:], axis=0)
    gram_c_own = jnp.dot(c_block.T, c_block, precision=HIGHEST)
    half = factor_b.shape[0] // 2
    second = share(
        jnp.concatenate(
            [
                jnp.concatenate([factor_b[:half], factor_b[half:]], axis=1),
                jnp.concatenate([gram_c_own, gram_b_pod], axis=1),
            ],
            axis=0,
        ),
        "pods",
        pods,
    )
    mixed = jnp.einsum("ijk,kr->ijr", tensor, c_block, precision=HIGHEST)
    b_block = jnp.stack([second[:, :half, :rank], second[:, :half, rank:]], axis=1).reshape(-1, rank)
    partial = jnp.sum(mixed * b_block[None], axis=1)
    everyone = share(partial.reshape(1, -1), ("racks", "pods"), racks * pods)
    grams = jnp.sum(second[:, half:], axis=0)
    lower = jnp.linalg.cholesky(grams[:, :rank] * grams[:, rank:])
    mttkrp = jnp.sum(everyone, axis=0).reshape(-1, rank)
    return jax.scipy.linalg.cho_solve((lower, True), mttkrp.T).T


def solution(mesh):
    in_specs = (P("rows", "racks", "pods"), P(("racks", "pods"), None), P(("pods", "racks"), None))
    out_specs = P("rows", None)
    return jax.shard_map(body, mesh=mesh, in_specs=in_specs, out_specs=out_specs, check_vma=False)
```

```python
import jax
import jax.numpy as jnp
from jax import lax
from jax.experimental import pallas as pl
from jax.experimental.pallas import tpu as pltpu
from jax.sharding import PartitionSpec as P

F32, BF16 = jnp.float32, jnp.bfloat16
VMEM = pl.BlockSpec(memory_space=pltpu.VMEM)
LIMIT = 40 * 1024 * 1024
ROWS = 512


def pieces(x, n):
    out = []
    for _ in range(n - 1):
        out.append(x.astype(BF16))
        x = x - out[-1].astype(F32)
    return out + [x.astype(BF16)]


def gram(x, dim):
    parts = pieces(x, 3)
    return sum(
        lax.dot_general(a, b, (((dim,), (dim,)), ((), ())), preferred_element_type=F32)
        for n, a in enumerate(parts)
        for b in parts[: 3 - n]
    )


def first_kernel(bt_ref, c_ref, out_ref):
    block = jnp.concatenate([c_ref[...], gram(bt_ref[...], 1)], axis=1)
    for n in range(out_ref.shape[0]):
        out_ref[n] = block


def second_kernel(bt_ref, in_ref, out_ref, w_ref):
    devices, rows, _ = in_ref.shape
    rank = bt_ref.shape[0]
    block = in_ref[...].reshape(devices * rows, 2 * rank)
    c = block[:, :rank]
    gram_b = jnp.sum(in_ref[...], axis=0)[:, rank:]
    grams = jnp.concatenate([gram(c, 0), gram_b], axis=1)
    half = bt_ref.shape[1] // 2
    b = jnp.concatenate([bt_ref[:, :half].T, bt_ref[:, half:].T], axis=1)
    for n in range(out_ref.shape[0]):
        out_ref[n, :half] = b
        out_ref[n, half:] = grams
    w_ref[...] = jnp.concatenate(pieces(c, 2), axis=1)


def mixed_kernel(t_ref, w_ref, out_ref):
    high, low = pieces(t_ref[0], 2)
    w = w_ref[...]
    both = jnp.dot(high, w, preferred_element_type=F32) + jnp.dot(low, w, preferred_element_type=F32)
    rank = w.shape[1] // 2
    both = both + pltpu.roll(both, rank, 1)
    left = lax.broadcasted_iota(jnp.int32, out_ref.shape[2:], 1) < rank
    half = out_ref.shape[2]
    for n in range(out_ref.shape[1]):
        at = 2 * half * n
        out_ref[0, n] = jnp.where(left, both[at : at + half], both[at + half : at + 2 * half])


def partial_kernel(mixed_ref, in_ref, out_ref):
    half = mixed_ref.shape[2]
    width = mixed_ref.shape[3]
    rows = []
    for i in range(2):
        total = jnp.zeros((8, width), F32)
        for n in range(mixed_ref.shape[1]):
            product = mixed_ref[i, n] * in_ref[n, :half]
            total = total + jnp.sum(product.reshape(half // 8, 8, width), axis=0)
        row = jnp.sum(total, axis=0, keepdims=True)
        rows.append(row + pltpu.roll(row, width // 2, 1))
    left = lax.broadcasted_iota(jnp.int32, (1, width), 1) < width // 2
    out_ref[...] = jnp.broadcast_to(jnp.where(left, rows[0], rows[1])[None], out_ref.shape)


def factor_kernel(in_ref, out_ref):
    rank = in_ref.shape[1] // 3
    grams = jnp.sum(in_ref[:, 2 * rank :], axis=0)
    a = grams[:, :rank] * grams[:, rank:]
    eye = lax.broadcasted_iota(jnp.int32, (rank, rank), 0) == lax.broadcasted_iota(jnp.int32, (rank, rank), 1)
    a = jnp.concatenate([a, eye.astype(F32)], axis=1)
    row_at = lax.broadcasted_iota(jnp.int32, a.shape, 0)
    for k in range(rank):
        row = a[k : k + 1]
        column = a[:, k : k + 1]
        scale = lax.rsqrt(row[:, k : k + 1])
        row = row * scale
        out_ref[k : k + 1] = row[:, rank:]
        a = jnp.where(row_at > k, a - (column * scale) * row, a)


def last_kernel(in_ref, inverse_ref, out_ref):
    rank = inverse_ref.shape[0]
    total = jnp.sum(in_ref[:, 0, :], axis=0, keepdims=True)
    x = jnp.concatenate([total[:, :rank], total[:, rank:]], axis=0)
    inverse = inverse_ref[...]
    x = lax.dot_general(x, inverse, (((1,), (1,)), ((), ())), precision=lax.Precision.HIGHEST, preferred_element_type=F32)
    out_ref[...] = jnp.dot(x, inverse, precision=lax.Precision.HIGHEST, preferred_element_type=F32)


def call(kernel, name, ins, outs, **more):
    many = isinstance(outs, list)
    return pl.pallas_call(
        kernel,
        name=name,
        in_specs=[VMEM] * ins,
        out_specs=[VMEM] * len(outs) if many else VMEM,
        out_shape=outs,
        compiler_params=pltpu.CompilerParams(vmem_limit_bytes=LIMIT),
        **more,
    )


def exchange(x, axes):
    return lax.all_to_all(x, axes, 0, 0, tiled=True)


def body(tensor, factor_b, factor_c):
    racks, pods = lax.axis_size("racks"), lax.axis_size("pods")
    slabs, extent_j, extent_k = tensor.shape
    own_b, rank = factor_b.shape
    own_c = factor_c.shape[0]
    half, width = own_b // 2, 2 * rank
    shape = jax.ShapeDtypeStruct
    bt = factor_b.T

    first = call(first_kernel, "first", 2, shape((racks, own_c, width), F32))(bt, factor_c)
    first = exchange(first, "racks")
    second, w = call(
        second_kernel, "second", 2, [shape((pods, half + rank, width), F32), shape((extent_k, width), BF16)]
    )(bt, first)
    second = exchange(second, "pods")
    chunks = ROWS // own_b
    mixed = pl.pallas_call(
        mixed_kernel,
        name="mixed",
        grid=(slabs, extent_j // ROWS),
        in_specs=[
            pl.BlockSpec((1, ROWS, extent_k), lambda i, j: (i, j, 0)),
            pl.BlockSpec((extent_k, width), lambda i, j: (0, 0)),
        ],
        out_specs=pl.BlockSpec((1, chunks, half, width), lambda i, j: (i, j, 0, 0)),
        out_shape=shape((slabs, pods, half, width), F32),
        compiler_params=pltpu.CompilerParams(vmem_limit_bytes=LIMIT),
        cost_estimate=pl.CostEstimate(
            flops=4 * tensor.size * width, bytes_accessed=4 * tensor.size, transcendentals=0
        ),
    )(tensor, w)
    partial = call(partial_kernel, "partial", 2, shape((racks * pods, 1, width), F32))(mixed, second)
    everyone = exchange(partial, ("racks", "pods"))
    inverse = call(
        factor_kernel,
        "factor",
        1,
        shape((rank, rank), F32),
        cost_estimate=pl.CostEstimate(flops=4_000_000_000, bytes_accessed=800_000, transcendentals=64),
    )(second)
    return call(last_kernel, "last", 2, shape((slabs, rank), F32))(everyone, inverse)


def solution(mesh):
    in_specs = (P("rows", "racks", "pods"), P(("racks", "pods"), None), P(("pods", "racks"), None))
    out_specs = P("rows", None)
    return jax.shard_map(body, mesh=mesh, in_specs=in_specs, out_specs=out_specs, check_vma=False)
```

```python
import jax
import jax.numpy as jnp
from jax import lax
from jax.experimental import pallas as pl
from jax.experimental.pallas import tpu as pltpu
from jax.sharding import PartitionSpec as P

F32, BF16 = jnp.float32, jnp.bfloat16
HIGHEST = lax.Precision.HIGHEST
VMEM = pl.BlockSpec(memory_space=pltpu.VMEM)
ANY = pl.BlockSpec(memory_space=pl.ANY)
LIMIT = 24 * 1024 * 1024
ROWS, SLOTS = 1024, 3


def pieces(x, n):
    out = []
    for _ in range(n - 1):
        out.append(x.astype(BF16))
        x = x - out[-1].astype(F32)
    return out + [x.astype(BF16)]


def product(x, y, dim):
    xs, ys = pieces(x, 3), pieces(y, 3)
    return sum(
        lax.dot_general(a, b, (((dim,), (dim,)), ((), ())), preferred_element_type=F32)
        for n, a in enumerate(xs)
        for b in ys[: 3 - n]
    )


def fold(x, axis=0):
    half = x.shape[axis] // 2
    index = [slice(None)] * x.ndim
    upper, lower = list(index), list(index)
    upper[axis], lower[axis] = slice(0, half), slice(half, None)
    return jnp.concatenate([x[tuple(upper)], x[tuple(lower)]], axis=-1)


def unfold(x):
    rank = x.shape[-1] // 2
    return jnp.concatenate([x[..., :rank], x[..., rank:]], axis=-2)


def quarter():
    return jnp.bitwise_xor(lax.axis_index("rows"), lax.axis_index("pods") % 2 * (lax.axis_size("rows") // 2))


def first_kernel(bt_ref, c_ref, out_ref, b_ref, bt, c, sems):
    copies = [
        pltpu.make_async_copy(source, to, sems.at[n]) for n, (source, to) in enumerate(((bt_ref, bt), (c_ref, c)))
    ]
    for copy in copies:
        copy.start()
    copies[0].wait()
    half = b_ref.shape[0]
    b_ref[...] = jnp.concatenate([bt[:, :half].T, bt[:, half:].T], axis=1)
    share = bt.shape[0] // lax.axis_size("rows")
    at = pl.ds(pl.multiple_of(quarter() * share, share), share)
    gram_b = fold(product(bt[at], bt[...], 1))
    copies[1].wait()
    block = jnp.concatenate([fold(c[...]), gram_b], axis=0)
    for n in range(out_ref.shape[0]):
        out_ref[n] = block


def second_kernel(b_ref, in_ref, out_ref, gram, grams, sems):
    rank = gram.shape[0]
    half, own = b_ref.shape[0], grams.shape[0] // 2
    rows = in_ref.shape[1] - own
    copies = []
    for n in range(out_ref.shape[0]):
        copies.append(pltpu.make_async_copy(b_ref, out_ref.at[n, pl.ds(0, half)], sems.at[0, n]))
        copies[-1].start()
    c = in_ref[:, :rows].reshape(-1, 2 * rank)
    both = product(c, c, 0)
    gram[...] = both[:rank, :rank] + both[rank:, rank:]
    at = pl.ds(pl.multiple_of(quarter() * 2 * own, 2 * own), 2 * own)
    grams[:own] = fold(gram[at])
    grams[own:] = jnp.sum(in_ref[:, rows:], axis=0)
    for n in range(out_ref.shape[0]):
        copies.append(pltpu.make_async_copy(grams, out_ref.at[n, pl.ds(half, 2 * own)], sems.at[1, n]))
        copies[-1].start()
    for copy in copies:
        copy.wait()


def mixed_kernel(t_ref, c_ref, out_ref, buffer, sems):
    slots, step, extent = buffer.shape
    devices, _, width = c_ref.shape
    rank = width // 2
    each = t_ref.shape[1] // step
    steps = t_ref.shape[0] * each

    def copy(n):
        at = pl.ds(pl.multiple_of(n % each * step, step), step)
        return pltpu.make_async_copy(t_ref.at[n // each, at], buffer.at[n % slots], sems.at[n % slots])

    for n in range(slots):
        copy(n).start()
    c = unfold(c_ref[:, : extent // devices // 2]).reshape(extent, rank)
    w = jnp.concatenate(pieces(c, 2), axis=1)
    half = out_ref.shape[2]
    left = lax.broadcasted_iota(jnp.int32, (half, width), 1) < rank

    def work(n, carry):
        copy(n).wait()
        high, low = pieces(buffer[n % slots], 2)
        both = jnp.dot(high, w, preferred_element_type=F32) + jnp.dot(low, w, preferred_element_type=F32)

        @pl.when(n + slots < steps)
        def _():
            copy(n + slots).start()

        both = both + pltpu.roll(both, rank, 1)
        for m in range(step // (2 * half)):
            part = both[2 * half * m : 2 * half * (m + 1)]
            out_ref[n // each, n % each * (step // (2 * half)) + m] = jnp.where(left, part[:half], part[half:])
        return carry

    lax.fori_loop(0, steps, work, 0)


def partial_kernel(mixed_ref, in_ref, out_ref):
    half = mixed_ref.shape[2]
    width = mixed_ref.shape[3]
    rows = []
    for i in range(2):
        total = jnp.zeros((8, width), F32)
        for n in range(mixed_ref.shape[1]):
            each = mixed_ref[i, n] * in_ref[n, :half]
            total = total + jnp.sum(each.reshape(half // 8, 8, width), axis=0)
        row = jnp.sum(total, axis=0, keepdims=True)
        rows.append(row + pltpu.roll(row, width // 2, 1))
    left = lax.broadcasted_iota(jnp.int32, (1, width), 1) < width // 2
    out_ref[...] = jnp.broadcast_to(jnp.where(left, rows[0], rows[1]), out_ref.shape)


def normal_kernel(in_ref, partial_ref, out_ref):
    own = out_ref.shape[0]
    grams = jnp.sum(in_ref[:, in_ref.shape[1] - 2 * own :], axis=0)
    out_ref[...] = grams[:own] * grams[own:]


def factor_kernel(*refs):
    parts, out_ref, (normal, inverse) = refs[:-3], refs[-3], refs[-2:]
    rank = normal.shape[0]
    share = rank // len(parts)
    me = quarter()
    for n, part in enumerate(parts):
        at = pl.ds(pl.multiple_of(jnp.bitwise_xor(me, n) * share, share), share)
        normal[at] = unfold(part[...])
    a = normal[...]
    eye = lax.broadcasted_iota(jnp.int32, (rank, rank), 0) == lax.broadcasted_iota(jnp.int32, (rank, rank), 1)
    a = jnp.concatenate([a, eye.astype(F32)], axis=1)
    row_at = lax.broadcasted_iota(jnp.int32, a.shape, 0)
    for k in range(rank):
        row = a[k : k + 1]
        column = a[:, k : k + 1]
        scale = lax.rsqrt(row[:, k : k + 1])
        row = row * scale
        inverse[k : k + 1] = row[:, rank:]
        a = jnp.where(row_at > k, a - (column * scale) * row, a)
    root = inverse[...]
    full = lax.dot_general(root, root, (((0,), (0,)), ((), ())), precision=HIGHEST, preferred_element_type=F32)
    out_ref[...] = jnp.concatenate(pieces(full, 3), axis=1)


def last_kernel(in_ref, inverse_ref, out_ref):
    rank = inverse_ref.shape[0]
    total = jnp.sum(in_ref[...], axis=0, keepdims=True)
    x = jnp.concatenate([total[:, :rank], total[:, rank:]], axis=0)
    parts = jnp.dot(jnp.concatenate(pieces(x, 3), axis=0), inverse_ref[...], preferred_element_type=F32)
    out_ref[...] = sum(
        parts[2 * n : 2 * n + 2, m * rank : (m + 1) * rank] for n in reversed(range(3)) for m in reversed(range(3 - n))
    )


def call(kernel, name, ins, outs, scratch=(), out=VMEM, **more):
    return pl.pallas_call(
        kernel,
        name=name,
        in_specs=ins,
        out_specs=out,
        out_shape=outs,
        scratch_shapes=scratch,
        compiler_params=pltpu.CompilerParams(vmem_limit_bytes=LIMIT),
        **more,
    )


def exchange(x, axes, groups=None):
    return lax.all_to_all(x, axes, 0, 0, tiled=True, axis_index_groups=groups)


def body(groups, tensor, factor_b, factor_c):
    rows, racks, pods = (lax.axis_size(axis) for axis in ("rows", "racks", "pods"))
    slabs, extent_j, extent_k = tensor.shape
    own_b, rank = factor_b.shape
    own_c = factor_c.shape[0]
    half, width, own = own_b // 2, 2 * rank, rank // rows // 2
    shape, fast = jax.ShapeDtypeStruct, pltpu.VMEM
    tensor, bt, factor_c = (pltpu.with_memory_space_constraint(x, pltpu.HBM) for x in (tensor, factor_b.T, factor_c))

    first, b = call(
        first_kernel,
        "first",
        [ANY, ANY],
        [fast((racks, own_c // 2 + own, width), F32), fast((half, width), F32)],
        [pltpu.VMEM(bt.shape, F32), pltpu.VMEM(factor_c.shape, F32), pltpu.SemaphoreType.DMA((2,))],
        [VMEM, VMEM],
    )(bt, factor_c)
    first = exchange(first, "racks")
    second = call(
        second_kernel,
        "second",
        [VMEM, VMEM],
        shape((pods, half + 2 * own, width), F32),
        [pltpu.VMEM((rank, rank), F32), pltpu.VMEM((2 * own, width), F32), pltpu.SemaphoreType.DMA((2, pods))],
        ANY,
    )(b, first)
    second = exchange(second, ("rows", "racks", "pods"), groups)
    mixed = call(
        mixed_kernel,
        "mixed",
        [ANY, VMEM],
        fast((slabs, pods, half, width), F32),
        [pltpu.VMEM((SLOTS, ROWS, extent_k), F32), pltpu.SemaphoreType.DMA((SLOTS,))],
        cost_estimate=pl.CostEstimate(
            flops=4 * tensor.size * width, bytes_accessed=4 * tensor.size, transcendentals=0
        ),
    )(tensor, first)
    partial = call(partial_kernel, "partial", [VMEM, VMEM], shape((racks * pods, width), F32))(mixed, second)
    everyone = exchange(partial.reshape(racks * pods, 1, width), ("racks", "pods"))
    normal = call(
        normal_kernel,
        "normal",
        [VMEM, ANY],
        shape((own, width), F32),
        cost_estimate=pl.CostEstimate(flops=1_000_000, bytes_accessed=80_000, transcendentals=0),
    )(second, partial)
    normals = [normal] + [lax.ppermute(normal, "rows", [(r, r ^ n) for r in range(rows)]) for n in range(1, rows)]
    inverse = call(
        factor_kernel,
        "factor",
        [VMEM] * rows,
        shape((rank, 3 * rank), BF16),
        [pltpu.VMEM((rank, rank), F32), pltpu.VMEM((rank, rank), F32)],
        cost_estimate=pl.CostEstimate(flops=1_000_000, bytes_accessed=80_000, transcendentals=64),
    )(*normals)
    return call(last_kernel, "last", [VMEM, VMEM], shape((slabs, rank), F32))(
        everyone.reshape(racks * pods, width), inverse
    )


def nearest_pods(mesh):
    rows, racks, pods = (mesh.shape[axis] for axis in ("rows", "racks", "pods"))
    return [
        [((low ^ (p % 2)) * (rows // 2) + core) * racks * pods + z * pods + p for p in range(pods)]
        for low in range(2)
        for core in range(rows // 2)
        for z in range(racks)
    ]


def solution(mesh):
    groups = nearest_pods(mesh)

    def mapped(tensor, factor_b, factor_c):
        return body(groups, tensor, factor_b, factor_c)

    in_specs = (P("rows", "racks", "pods"), P(("racks", "pods"), None), P(("pods", "racks"), None))
    out_specs = P("rows", None)
    return jax.shard_map(mapped, mesh=mesh, in_specs=in_specs, out_specs=out_specs, check_vma=False)
```

```python
import functools

import jax
import jax.numpy as jnp
from jax import lax
from jax.experimental import pallas as pl
from jax.experimental.pallas import tpu as pltpu
from jax.sharding import PartitionSpec as P

F32, BF16 = jnp.float32, jnp.bfloat16
HIGHEST = lax.Precision.HIGHEST
VMEM = pl.BlockSpec(memory_space=pltpu.VMEM)
ANY = pl.BlockSpec(memory_space=pl.ANY)
LIMIT = 24 * 1024 * 1024
ROWS, SLOTS = 1024, 3
EARLY = 96


def pieces(x, n):
    out = []
    for _ in range(n - 1):
        out.append(x.astype(BF16))
        x = x - out[-1].astype(F32)
    return out + [x.astype(BF16)]


def product(x, y, dim):
    xs, ys = pieces(x, 3), pieces(y, 3)
    return sum(
        lax.dot_general(a, b, (((dim,), (dim,)), ((), ())), preferred_element_type=F32)
        for n, a in enumerate(xs)
        for b in ys[: 3 - n]
    )


def fold(x, axis=0):
    half = x.shape[axis] // 2
    index = [slice(None)] * x.ndim
    upper, lower = list(index), list(index)
    upper[axis], lower[axis] = slice(0, half), slice(half, None)
    return jnp.concatenate([x[tuple(upper)], x[tuple(lower)]], axis=-1)


def unfold(x):
    rank = x.shape[-1] // 2
    return jnp.concatenate([x[..., :rank], x[..., rank:]], axis=-2)


def half_label():
    return jnp.bitwise_xor(lax.axis_index("rows") // 2, lax.axis_index("pods") % 2)


def gathers_b():
    return lax.axis_index("rows") % 2 == 0


def first_kernel(bt_ref, c_ref, out_ref, b_ref, bt, c, sems):
    copies = [
        pltpu.make_async_copy(source, to, sems.at[n]) for n, (source, to) in enumerate(((bt_ref, bt), (c_ref, c)))
    ]
    for copy in copies:
        copy.start()
    copies[0].wait()
    half = b_ref.shape[0]
    b_ref[...] = jnp.concatenate([bt[:, :half].T, bt[:, half:].T], axis=1)
    share = bt.shape[0] // 2
    at = pl.ds(pl.multiple_of(half_label() * share, share), share)
    gram_b = fold(product(bt[at], bt[...], 1))
    copies[1].wait()
    other = jnp.concatenate([fold(c[...]), gram_b], axis=0)
    rows = out_ref.shape[1]
    other = jnp.concatenate([other, jnp.zeros((rows - other.shape[0], other.shape[1]), F32)], axis=0)
    block = jnp.where(gathers_b(), b_ref[:rows], other)
    for n in range(out_ref.shape[0]):
        out_ref[n] = block


def second_kernel(rows, b_ref, in_ref, out_ref, gram, grams, sems):
    rank = gram.shape[0]
    own = grams.shape[0] // 2
    first = in_ref.shape[1]
    rest = b_ref.shape[0] - first
    copies = []
    for n in range(out_ref.shape[0]):
        copies.append(
            pltpu.make_async_copy(b_ref.at[pl.ds(first, rest)], out_ref.at[n, pl.ds(0, rest)], sems.at[0, n])
        )
        copies[-1].start()
    c = in_ref[:, :rows].reshape(-1, 2 * rank)
    both = product(c, c, 0)
    gram[...] = both[:rank, :rank] + both[rank:, rank:]
    at = pl.ds(pl.multiple_of(half_label() * 2 * own, 2 * own), 2 * own)
    grams[:own] = fold(gram[at])
    grams[own:] = jnp.sum(in_ref[:, rows : rows + own], axis=0)
    for n in range(out_ref.shape[0]):
        copies.append(pltpu.make_async_copy(grams, out_ref.at[n, pl.ds(rest, 2 * own)], sems.at[1, n]))
        copies[-1].start()
    for copy in copies:
        copy.wait()


def mixed_kernel(t_ref, own_ref, other_ref, out_ref, buffer, sems):
    slots, step, extent = buffer.shape
    devices, _, width = own_ref.shape
    rank = width // 2
    each = t_ref.shape[1] // step
    steps = t_ref.shape[0] * each

    def copy(n):
        at = pl.ds(pl.multiple_of(n % each * step, step), step)
        return pltpu.make_async_copy(t_ref.at[n // each, at], buffer.at[n % slots], sems.at[n % slots])

    for n in range(slots):
        copy(n).start()
    rows = extent // devices // 2
    c = jnp.where(gathers_b(), other_ref[:, :rows], own_ref[:, :rows])
    c = unfold(c).reshape(extent, rank)
    w = jnp.concatenate(pieces(c, 2), axis=1)
    half = out_ref.shape[2]
    left = lax.broadcasted_iota(jnp.int32, (half, width), 1) < rank

    def work(n, carry):
        copy(n).wait()
        high, low = pieces(buffer[n % slots], 2)
        both = jnp.dot(high, w, preferred_element_type=F32) + jnp.dot(low, w, preferred_element_type=F32)

        @pl.when(n + slots < steps)
        def _():
            copy(n + slots).start()

        both = both + pltpu.roll(both, rank, 1)
        for m in range(step // (2 * half)):
            part = both[2 * half * m : 2 * half * (m + 1)]
            out_ref[n // each, n % each * (step // (2 * half)) + m] = jnp.where(left, part[:half], part[half:])
        return carry

    lax.fori_loop(0, steps, work, 0)


def partial_kernel(mixed_ref, own_ref, other_ref, in_ref, out_ref):
    half = mixed_ref.shape[2]
    width = mixed_ref.shape[3]
    first = own_ref.shape[1]
    mine = gathers_b()
    totals = [jnp.zeros((8, width), F32) for _ in range(2)]
    for n in range(mixed_ref.shape[1]):
        b = jnp.where(mine, own_ref[n], other_ref[n])
        b = jnp.concatenate([b, in_ref[n, : half - first]], axis=0)
        for i in range(2):
            totals[i] = totals[i] + jnp.sum((mixed_ref[i, n] * b).reshape(half // 8, 8, width), axis=0)
    rows = []
    for total in totals:
        row = jnp.sum(total, axis=0, keepdims=True)
        rows.append(row + pltpu.roll(row, width // 2, 1))
    left = lax.broadcasted_iota(jnp.int32, (1, width), 1) < width // 2
    out_ref[...] = jnp.broadcast_to(jnp.where(left, rows[0], rows[1]), out_ref.shape)


def normal_kernel(in_ref, partial_ref, out_ref):
    own = out_ref.shape[0]
    grams = jnp.sum(in_ref[:, in_ref.shape[1] - 2 * own :], axis=0)
    out_ref[...] = grams[:own] * grams[own:]


def factor_kernel(*refs):
    parts, out_ref, (normal, inverse) = refs[:-3], refs[-3], refs[-2:]
    rank = normal.shape[0]
    share = rank // 2
    me = half_label()
    own, core, chip, both = (part[...] for part in parts)
    for n, part in enumerate((jnp.where(gathers_b(), core, own), jnp.where(gathers_b(), both, chip))):
        at = pl.ds(pl.multiple_of(jnp.bitwise_xor(me, n) * share, share), share)
        normal[at] = unfold(part)
    a = normal[...]
    eye = lax.broadcasted_iota(jnp.int32, (rank, rank), 0) == lax.broadcasted_iota(jnp.int32, (rank, rank), 1)
    a = jnp.concatenate([a, eye.astype(F32)], axis=1)
    row_at = lax.broadcasted_iota(jnp.int32, a.shape, 0)
    for k in range(rank):
        row = a[k : k + 1]
        column = a[:, k : k + 1]
        scale = lax.rsqrt(row[:, k : k + 1])
        row = row * scale
        inverse[k : k + 1] = row[:, rank:]
        a = jnp.where(row_at > k, a - (column * scale) * row, a)
    root = inverse[...]
    full = lax.dot_general(root, root, (((0,), (0,)), ((), ())), precision=HIGHEST, preferred_element_type=F32)
    out_ref[...] = jnp.concatenate(pieces(full, 3), axis=1)


def last_kernel(in_ref, inverse_ref, out_ref):
    rank = inverse_ref.shape[0]
    total = jnp.sum(in_ref[...], axis=0, keepdims=True)
    x = jnp.concatenate([total[:, :rank], total[:, rank:]], axis=0)
    parts = jnp.dot(jnp.concatenate(pieces(x, 3), axis=0), inverse_ref[...], preferred_element_type=F32)
    out_ref[...] = sum(
        parts[2 * n : 2 * n + 2, m * rank : (m + 1) * rank] for n in reversed(range(3)) for m in reversed(range(3 - n))
    )


def call(kernel, name, ins, outs, scratch=(), out=VMEM, **more):
    return pl.pallas_call(
        kernel,
        name=name,
        in_specs=ins,
        out_specs=out,
        out_shape=outs,
        scratch_shapes=scratch,
        compiler_params=pltpu.CompilerParams(vmem_limit_bytes=LIMIT),
        **more,
    )


def exchange(x, axes, groups=None):
    return lax.all_to_all(x, axes, 0, 0, tiled=True, axis_index_groups=groups)


def body(gather_groups, pods_groups, tensor, factor_b, factor_c):
    axes = ("rows", "racks", "pods")
    rows, racks, pods = (lax.axis_size(axis) for axis in axes)
    slabs, extent_j, extent_k = tensor.shape
    own_b, rank = factor_b.shape
    own_c = factor_c.shape[0]
    half, width, own = own_b // 2, 2 * rank, rank // 4
    shape, fast = jax.ShapeDtypeStruct, pltpu.VMEM
    tensor, bt, factor_c = (pltpu.with_memory_space_constraint(x, pltpu.HBM) for x in (tensor, factor_b.T, factor_c))

    first, b = call(
        first_kernel,
        "first",
        [ANY, ANY],
        [fast((racks, EARLY, width), F32), fast((half, width), F32)],
        [pltpu.VMEM(bt.shape, F32), pltpu.VMEM(factor_c.shape, F32), pltpu.SemaphoreType.DMA((2,))],
        [VMEM, VMEM],
    )(bt, factor_c)
    first = exchange(first, axes, gather_groups)
    other = lax.ppermute(first, "rows", [(r, r ^ 1) for r in range(rows)])
    second = call(
        functools.partial(second_kernel, own_c // 2),
        "second",
        [VMEM, VMEM],
        shape((pods, half - EARLY + 2 * own, width), F32),
        [pltpu.VMEM((rank, rank), F32), pltpu.VMEM((2 * own, width), F32), pltpu.SemaphoreType.DMA((2, pods))],
        ANY,
    )(b, first)
    second = exchange(second, axes, pods_groups)
    mixed = call(
        mixed_kernel,
        "mixed",
        [ANY, VMEM, VMEM],
        fast((slabs, pods, half, width), F32),
        [pltpu.VMEM((SLOTS, ROWS, extent_k), F32), pltpu.SemaphoreType.DMA((SLOTS,))],
        cost_estimate=pl.CostEstimate(
            flops=4 * tensor.size * width, bytes_accessed=4 * tensor.size, transcendentals=0
        ),
    )(tensor, first, other)
    partial = call(partial_kernel, "partial", [VMEM] * 4, shape((racks * pods, width), F32))(
        mixed, first, other, second
    )
    everyone = exchange(partial.reshape(racks * pods, 1, width), ("racks", "pods"))
    normal = call(
        normal_kernel,
        "normal",
        [VMEM, ANY],
        shape((own, width), F32),
        cost_estimate=pl.CostEstimate(flops=1_000_000, bytes_accessed=80_000, transcendentals=0),
    )(second, partial)
    normals = [normal] + [lax.ppermute(normal, "rows", [(r, r ^ n) for r in range(rows)]) for n in range(1, rows)]
    inverse = call(
        factor_kernel,
        "factor",
        [VMEM] * rows,
        shape((rank, 3 * rank), BF16),
        [pltpu.VMEM((rank, rank), F32), pltpu.VMEM((rank, rank), F32)],
        cost_estimate=pl.CostEstimate(flops=1_000_000, bytes_accessed=80_000, transcendentals=64),
    )(*normals)
    return call(last_kernel, "last", [VMEM, VMEM], shape((slabs, rank), F32))(
        everyone.reshape(racks * pods, width), inverse
    )


def groups_of(mesh):
    rows, racks, pods = (mesh.shape[axis] for axis in ("rows", "racks", "pods"))

    def device(low, core, z, p):
        return ((low * 2 + core) * racks + z) * pods + p

    lows = range(rows // 2)
    by_pods = [
        [[device(low ^ (p % 2), core, z, p) for p in range(pods)] for low in lows for z in range(racks)] for core in range(2)
    ]
    by_racks = [[device(low, 1, z, p) for z in range(racks)] for low in lows for p in range(pods)]
    return by_pods[0] + by_racks, by_pods[0] + by_pods[1]


def solution(mesh):
    groups = groups_of(mesh)

    def mapped(tensor, factor_b, factor_c):
        return body(*groups, tensor, factor_b, factor_c)

    in_specs = (P("rows", "racks", "pods"), P(("racks", "pods"), None), P(("pods", "racks"), None))
    out_specs = P("rows", None)
    return jax.shard_map(mapped, mesh=mesh, in_specs=in_specs, out_specs=out_specs, check_vma=False)
```

```python
import jax
import jax.numpy as jnp
from jax import lax
from jax.experimental import pallas as pl
from jax.experimental.pallas import tpu as pltpu
from jax.sharding import PartitionSpec as P

F32, BF16 = jnp.float32, jnp.bfloat16
HIGHEST = lax.Precision.HIGHEST
VMEM = pl.BlockSpec(memory_space=pltpu.VMEM)
ANY = pl.BlockSpec(memory_space=pl.ANY)
LIMIT = 24 * 1024 * 1024
ROWS, SLOTS = 1024, 3


def pieces(x, n):
    out = []
    for _ in range(n - 1):
        out.append(x.astype(BF16))
        x = x - out[-1].astype(F32)
    return out + [x.astype(BF16)]


def product(x, y, dim):
    (a, b, c), (d, e, f) = pieces(x, 3), pieces(y, 3)
    left = jnp.concatenate([a, a, a, b, b, c], axis=dim)
    right = jnp.concatenate([d, e, f, d, e, d], axis=dim)
    return lax.dot_general(left, right, (((dim,), (dim,)), ((), ())), preferred_element_type=F32)


def fold(x, axis=0):
    half = x.shape[axis] // 2
    index = [slice(None)] * x.ndim
    upper, lower = list(index), list(index)
    upper[axis], lower[axis] = slice(0, half), slice(half, None)
    return jnp.concatenate([x[tuple(upper)], x[tuple(lower)]], axis=-1)


def unfold(x):
    rank = x.shape[-1] // 2
    return jnp.concatenate([x[..., :rank], x[..., rank:]], axis=-2)


def gathers_b():
    return lax.axis_index("rows") % 2 == 0


def first_kernel(bt_ref, c_ref, out_ref, bt, c, sems):
    copies = [
        pltpu.make_async_copy(source, to, sems.at[n]) for n, (source, to) in enumerate(((bt_ref, bt), (c_ref, c)))
    ]
    for copy in copies:
        copy.start()
    for copy in copies:
        copy.wait()
    rows = out_ref.shape[1]

    def send(block):
        for n in range(out_ref.shape[0]):
            out_ref[n, : block.shape[0]] = block

    @pl.when(gathers_b())
    def _():
        send(jnp.concatenate([bt[:, :rows].T, bt[:, rows:].T], axis=1))

    @pl.when(jnp.logical_not(gathers_b()))
    def _():
        grams = [fold(product(bt[...], bt[...], 1)), fold(product(c[...], c[...], 0))]
        block = jnp.concatenate([fold(c[...]), *grams], axis=0)
        send(jnp.concatenate([block, jnp.zeros((rows - block.shape[0], block.shape[1]), F32)], axis=0))


def grams_kernel(in_ref, out_ref):
    rows = out_ref.shape[0]
    out_ref[...] = jnp.sum(in_ref[:, rows // 2 : rows // 2 + rows], axis=0)


def add_kernel(x_ref, y_ref, after_ref, out_ref):
    total = x_ref[...] + y_ref[...]
    rows = out_ref.shape[0]
    out_ref[...] = total if total.shape[0] == rows else total[:rows] * total[rows:]


def mixed_kernel(t_ref, own_ref, other_ref, out_ref, buffer, sems):
    slots, step, extent = buffer.shape
    devices, _, width = own_ref.shape
    rank = width // 2
    each = t_ref.shape[1] // step
    steps = t_ref.shape[0] * each

    def copy(n):
        at = pl.ds(pl.multiple_of(n % each * step, step), step)
        return pltpu.make_async_copy(t_ref.at[n // each, at], buffer.at[n % slots], sems.at[n % slots])

    for n in range(slots):
        copy(n).start()
    rows = extent // devices // 2
    c = jnp.where(gathers_b(), other_ref[:, :rows], own_ref[:, :rows])
    c = unfold(c).reshape(extent, rank)
    w = jnp.concatenate(pieces(c, 2), axis=1)
    half = out_ref.shape[2]
    left = lax.broadcasted_iota(jnp.int32, (half, width), 1) < rank

    def work(n, carry):
        copy(n).wait()
        high, low = pieces(buffer[n % slots], 2)
        both = jnp.dot(high, w, preferred_element_type=F32) + jnp.dot(low, w, preferred_element_type=F32)

        @pl.when(n + slots < steps)
        def _():
            copy(n + slots).start()

        both = both + pltpu.roll(both, rank, 1)
        for m in range(step // (2 * half)):
            part = both[2 * half * m : 2 * half * (m + 1)]
            out_ref[n // each, n % each * (step // (2 * half)) + m] = jnp.where(left, part[:half], part[half:])
        return carry

    lax.fori_loop(0, steps, work, 0)


def partial_kernel(mixed_ref, own_ref, other_ref, out_ref):
    half = mixed_ref.shape[2]
    width = mixed_ref.shape[3]
    mine = gathers_b()
    totals = [jnp.zeros((8, width), F32) for _ in range(2)]
    for n in range(mixed_ref.shape[1]):
        b = jnp.where(mine, own_ref[n], other_ref[n])
        for i in range(2):
            totals[i] = totals[i] + jnp.sum((mixed_ref[i, n] * b).reshape(half // 8, 8, width), axis=0)
    rows = []
    for total in totals:
        row = jnp.sum(total, axis=0, keepdims=True)
        rows.append(row + pltpu.roll(row, width // 2, 1))
    left = lax.broadcasted_iota(jnp.int32, (1, width), 1) < width // 2
    out_ref[...] = jnp.broadcast_to(jnp.where(left, rows[0], rows[1]), out_ref.shape)


def factor_kernel(own_ref, other_ref, out_ref, inverse):
    rank = inverse.shape[0]
    a = unfold(jnp.where(gathers_b(), other_ref[...], own_ref[...]))
    eye = lax.broadcasted_iota(jnp.int32, (rank, rank), 0) == lax.broadcasted_iota(jnp.int32, (rank, rank), 1)
    a = jnp.concatenate([a, eye.astype(F32)], axis=1)
    tile = 8
    tiles = [a[n : n + tile] for n in range(0, rank, tile)]

    def lanes(x, n):
        return jnp.broadcast_to(x[:, n : n + 1], x.shape)

    def sublanes(x, n):
        return jnp.broadcast_to(x[n : n + 1], x.shape)

    for t in range(len(tiles)):
        below = range(t, len(tiles))
        columns = {u: [lanes(tiles[u], tile * t + j) for j in range(tile)] for u in below}
        rows = [sublanes(tiles[t], j) for j in range(tile)]
        for j in range(tile):
            scale = lax.rsqrt(sublanes(columns[t][j], j))
            rows[j] = rows[j] * scale
            inverse[tile * t + j : tile * t + j + 1] = rows[j][:1, rank:]
            for u in below:
                columns[u][j] = columns[u][j] * scale
            for m in range(j + 1, tile):
                pivot = sublanes(columns[t][j], m)
                rows[m] = rows[m] - pivot * rows[j]
                for u in below:
                    columns[u][m] = columns[u][m] - columns[u][j] * pivot
        for u in below[1:]:
            for j in range(tile):
                tiles[u] = tiles[u] - columns[u][j] * rows[j]
    root = inverse[...]
    full = lax.dot_general(root, root, (((0,), (0,)), ((), ())), precision=HIGHEST, preferred_element_type=F32)
    out_ref[...] = jnp.concatenate(pieces(full, 3), axis=1)


def last_kernel(in_ref, inverse_ref, out_ref):
    rank = inverse_ref.shape[0]
    total = jnp.sum(in_ref[...], axis=0, keepdims=True)
    x = jnp.concatenate([total[:, :rank], total[:, rank:]], axis=0)
    parts = jnp.dot(jnp.concatenate(pieces(x, 3), axis=0), inverse_ref[...], preferred_element_type=F32)
    out_ref[...] = sum(
        parts[2 * n : 2 * n + 2, m * rank : (m + 1) * rank] for n in reversed(range(3)) for m in reversed(range(3 - n))
    )


def call(kernel, name, ins, outs, scratch=(), out=VMEM, **more):
    return pl.pallas_call(
        kernel,
        name=name,
        in_specs=ins,
        out_specs=out,
        out_shape=outs,
        scratch_shapes=scratch,
        compiler_params=pltpu.CompilerParams(vmem_limit_bytes=LIMIT),
        **more,
    )


def body(pairs, gather_groups, tensor, factor_b, factor_c):
    axes = ("rows", "racks", "pods")
    racks, pods = lax.axis_size("racks"), lax.axis_size("pods")
    slabs, _, extent_k = tensor.shape
    own_b, rank = factor_b.shape
    half, width = own_b // 2, 2 * rank
    shape, fast = jax.ShapeDtypeStruct, pltpu.VMEM
    tensor, bt, factor_c = (pltpu.with_memory_space_constraint(x, pltpu.HBM) for x in (tensor, factor_b.T, factor_c))
    small = pl.CostEstimate(flops=1_000_000, bytes_accessed=80_000, transcendentals=64)

    first = call(
        first_kernel,
        "first",
        [ANY, ANY],
        fast((racks, half, width), F32),
        [pltpu.VMEM(bt.shape, F32), pltpu.VMEM(factor_c.shape, F32), pltpu.SemaphoreType.DMA((2,))],
    )(bt, factor_c)
    first = lax.all_to_all(first, axes, 0, 0, tiled=True, axis_index_groups=gather_groups)
    chip = [(r, r ^ 1) for r in range(lax.axis_size("rows"))]
    other = lax.ppermute(first, "rows", chip)
    grams = call(grams_kernel, "grams", [VMEM], shape((rank, width), F32), cost_estimate=small)(first)
    mixed = call(
        mixed_kernel,
        "mixed",
        [ANY, VMEM, VMEM],
        fast((slabs, pods, half, width), F32),
        [pltpu.VMEM((SLOTS, ROWS, extent_k), F32), pltpu.SemaphoreType.DMA((SLOTS,))],
        cost_estimate=pl.CostEstimate(
            flops=4 * tensor.size * width, bytes_accessed=4 * tensor.size, transcendentals=0
        ),
    )(tensor, first, other)
    partial = call(partial_kernel, "partial", [VMEM] * 3, shape((racks * pods, width), F32))(mixed, first, other)
    for step, (pair, after) in enumerate(zip(pairs, (mixed, partial, partial), strict=True)):
        arrived = lax.ppermute(grams, axes, pair)
        rows = rank if step + 1 < len(pairs) else rank // 2
        grams = call(add_kernel, f"add{step}", [VMEM, VMEM, ANY], shape((rows, width), F32), cost_estimate=small)(
            grams, arrived, after
        )
    everyone = lax.all_to_all(partial.reshape(racks * pods, 1, width), ("racks", "pods"), 0, 0, tiled=True)
    inverse = call(
        factor_kernel,
        "factor",
        [VMEM] * 2,
        shape((rank, 3 * rank), BF16),
        [pltpu.VMEM((rank, rank), F32)],
        cost_estimate=small,
    )(grams, lax.ppermute(grams, "rows", chip))
    return call(last_kernel, "last", [VMEM, VMEM], shape((slabs, rank), F32))(
        everyone.reshape(racks * pods, width), inverse
    )


def routes(mesh):
    rows, racks, pods = (mesh.shape[axis] for axis in ("rows", "racks", "pods"))

    def device(low, core, z, p):
        return ((low * 2 + core) * racks + z) * pods + p

    every = [(low, z, p) for low in range(rows // 2) for z in range(racks) for p in range(pods)]
    pairs = [
        [(device(low, 1, z, p), device(to(low, p)[0], 1, z, to(low, p)[1])) for low, z, p in every]
        for to in (lambda low, p: (low ^ 1, p ^ 1), lambda low, p: (low, p ^ 2), lambda low, p: (low, p ^ 6))
    ]
    by_pods = [[device(low ^ (p % 2), 0, z, p) for p in range(pods)] for low in range(rows // 2) for z in range(racks)]
    by_racks = [[device(low, 1, z, p) for z in range(racks)] for low in range(rows // 2) for p in range(pods)]
    return pairs, by_pods + by_racks


def solution(mesh):
    pairs, groups = routes(mesh)

    def mapped(tensor, factor_b, factor_c):
        return body(pairs, groups, tensor, factor_b, factor_c)

    in_specs = (P("rows", "racks", "pods"), P(("racks", "pods"), None), P(("pods", "racks"), None))
    out_specs = P("rows", None)
    return jax.shard_map(mapped, mesh=mesh, in_specs=in_specs, out_specs=out_specs, check_vma=False)
```

```python
import jax
import jax.numpy as jnp
from jax import lax
from jax.experimental import pallas as pl
from jax.experimental.pallas import tpu as pltpu
from jax.sharding import PartitionSpec as P

F32, BF16 = jnp.float32, jnp.bfloat16
HIGHEST = lax.Precision.HIGHEST
VMEM = pl.BlockSpec(memory_space=pltpu.VMEM)
ANY = pl.BlockSpec(memory_space=pl.ANY)
LIMIT = 24 * 1024 * 1024
ROWS, SLOTS = 1024, 3


def pieces(x, n):
    out = []
    for _ in range(n - 1):
        out.append(x.astype(BF16))
        x = x - out[-1].astype(F32)
    return out + [x.astype(BF16)]


def product(x, y, dim):
    (a, b, c), (d, e, f) = pieces(x, 3), pieces(y, 3)
    left = jnp.concatenate([a, a, a, b, b, c], axis=dim)
    right = jnp.concatenate([d, e, f, d, e, d], axis=dim)
    return lax.dot_general(left, right, (((dim,), (dim,)), ((), ())), preferred_element_type=F32)


def fold(x, axis=0):
    half = x.shape[axis] // 2
    index = [slice(None)] * x.ndim
    upper, lower = list(index), list(index)
    upper[axis], lower[axis] = slice(0, half), slice(half, None)
    return jnp.concatenate([x[tuple(upper)], x[tuple(lower)]], axis=-1)


def unfold(x):
    rank = x.shape[-1] // 2
    return jnp.concatenate([x[..., :rank], x[..., rank:]], axis=-2)


def gathers_b():
    return lax.axis_index("rows") % 2 == 0


def first_kernel(bt_ref, c_ref, out_ref, bt, c, sems):
    copies = [
        pltpu.make_async_copy(source, to, sems.at[n]) for n, (source, to) in enumerate(((bt_ref, bt), (c_ref, c)))
    ]
    for copy in copies:
        copy.start()
    for copy in copies:
        copy.wait()
    rows = out_ref.shape[1]

    def send(block):
        for n in range(out_ref.shape[0]):
            out_ref[n, : block.shape[0]] = block

    @pl.when(gathers_b())
    def _():
        send(jnp.concatenate([bt[:, :rows].T, bt[:, rows:].T], axis=1))

    @pl.when(jnp.logical_not(gathers_b()))
    def _():
        grams = [fold(product(bt[...], bt[...], 1)), fold(product(c[...], c[...], 0))]
        block = jnp.concatenate([fold(c[...]), *grams], axis=0)
        send(jnp.concatenate([block, jnp.zeros((rows - block.shape[0], block.shape[1]), F32)], axis=0))


def grams_kernel(own_ref, other_ref, out_ref):
    rows = out_ref.shape[0]
    at = slice(rows // 2, rows // 2 + rows)
    out_ref[...] = jnp.sum(jnp.where(gathers_b(), other_ref[:, at], own_ref[:, at]), axis=0)


def add_kernel(x_ref, y_ref, after_ref, out_ref):
    out_ref[...] = x_ref[...] + y_ref[...]


def mixed_kernel(t_ref, own_ref, other_ref, out_ref, buffer, sems):
    slots, step, extent = buffer.shape
    devices, _, width = own_ref.shape
    rank = width // 2
    each = t_ref.shape[1] // step
    steps = t_ref.shape[0] * each

    def copy(n):
        at = pl.ds(pl.multiple_of(n % each * step, step), step)
        return pltpu.make_async_copy(t_ref.at[n // each, at], buffer.at[n % slots], sems.at[n % slots])

    for n in range(slots):
        copy(n).start()
    rows = extent // devices // 2
    c = jnp.where(gathers_b(), other_ref[:, :rows], own_ref[:, :rows])
    c = unfold(c).reshape(extent, rank)
    w = jnp.concatenate(pieces(c, 2), axis=1)
    half = out_ref.shape[2]
    left = lax.broadcasted_iota(jnp.int32, (half, width), 1) < rank

    def work(n, carry):
        copy(n).wait()
        high, low = pieces(buffer[n % slots], 2)
        both = jnp.dot(high, w, preferred_element_type=F32) + jnp.dot(low, w, preferred_element_type=F32)

        @pl.when(n + slots < steps)
        def _():
            copy(n + slots).start()

        both = both + pltpu.roll(both, rank, 1)
        for m in range(step // (2 * half)):
            part = both[2 * half * m : 2 * half * (m + 1)]
            out_ref[n // each, n % each * (step // (2 * half)) + m] = jnp.where(left, part[:half], part[half:])
        return carry

    lax.fori_loop(0, steps, work, 0)


def partial_kernel(mixed_ref, own_ref, other_ref, out_ref):
    half = mixed_ref.shape[2]
    width = mixed_ref.shape[3]
    mine = gathers_b()
    totals = [jnp.zeros((8, width), F32) for _ in range(2)]
    for n in range(mixed_ref.shape[1]):
        b = jnp.where(mine, own_ref[n], other_ref[n])
        for i in range(2):
            totals[i] = totals[i] + jnp.sum((mixed_ref[i, n] * b).reshape(half // 8, 8, width), axis=0)
    rows = []
    for total in totals:
        row = jnp.sum(total, axis=0, keepdims=True)
        rows.append(row + pltpu.roll(row, width // 2, 1))
    left = lax.broadcasted_iota(jnp.int32, (1, width), 1) < width // 2
    out_ref[...] = jnp.broadcast_to(jnp.where(left, rows[0], rows[1]), out_ref.shape)


def factor_kernel(*refs):
    parts, out_ref, (grams, inverse) = refs[:-3], refs[-3], refs[-2:]
    rank = inverse.shape[0]
    for n, part in enumerate(parts):
        grams[jnp.bitwise_xor(lax.axis_index("pods") // 2, n)] = part[...]
    both = grams[0]
    for n in range(1, len(parts)):
        both = both + grams[n]
    a = unfold(both[: rank // 2] * both[rank // 2 :])
    eye = lax.broadcasted_iota(jnp.int32, (rank, rank), 0) == lax.broadcasted_iota(jnp.int32, (rank, rank), 1)
    a = jnp.concatenate([a, eye.astype(F32)], axis=1)
    tile = 8
    tiles = [a[n : n + tile] for n in range(0, rank, tile)]

    def lanes(x, n):
        return jnp.broadcast_to(x[:, n : n + 1], x.shape)

    def sublanes(x, n):
        return jnp.broadcast_to(x[n : n + 1], x.shape)

    for t in range(len(tiles)):
        below = range(t, len(tiles))
        columns = {u: [lanes(tiles[u], tile * t + j) for j in range(tile)] for u in below}
        rows = [sublanes(tiles[t], j) for j in range(tile)]
        for j in range(tile):
            scale = lax.rsqrt(sublanes(columns[t][j], j))
            rows[j] = rows[j] * scale
            inverse[tile * t + j : tile * t + j + 1] = rows[j][:1, rank:]
            for u in below:
                columns[u][j] = columns[u][j] * scale
            for m in range(j + 1, tile):
                pivot = sublanes(columns[t][j], m)
                rows[m] = rows[m] - pivot * rows[j]
                for u in below:
                    columns[u][m] = columns[u][m] - columns[u][j] * pivot
        for u in below[1:]:
            for j in range(tile):
                tiles[u] = tiles[u] - columns[u][j] * rows[j]
    root = inverse[...]
    full = lax.dot_general(root, root, (((0,), (0,)), ((), ())), precision=HIGHEST, preferred_element_type=F32)
    out_ref[...] = jnp.concatenate(pieces(full, 3), axis=1)


def last_kernel(in_ref, inverse_ref, out_ref):
    rank = inverse_ref.shape[0]
    total = jnp.sum(in_ref[...], axis=0, keepdims=True)
    x = jnp.concatenate([total[:, :rank], total[:, rank:]], axis=0)
    parts = jnp.dot(jnp.concatenate(pieces(x, 3), axis=0), inverse_ref[...], preferred_element_type=F32)
    out_ref[...] = sum(
        parts[2 * n : 2 * n + 2, m * rank : (m + 1) * rank] for n in reversed(range(3)) for m in reversed(range(3 - n))
    )


def call(kernel, name, ins, outs, scratch=(), out=VMEM, **more):
    return pl.pallas_call(
        kernel,
        name=name,
        in_specs=ins,
        out_specs=out,
        out_shape=outs,
        scratch_shapes=scratch,
        compiler_params=pltpu.CompilerParams(vmem_limit_bytes=LIMIT),
        **more,
    )


def body(pairs, gather_groups, tensor, factor_b, factor_c):
    axes = ("rows", "racks", "pods")
    racks, pods = lax.axis_size("racks"), lax.axis_size("pods")
    slabs, _, extent_k = tensor.shape
    own_b, rank = factor_b.shape
    half, width = own_b // 2, 2 * rank
    shape, fast = jax.ShapeDtypeStruct, pltpu.VMEM
    tensor, bt, factor_c = (pltpu.with_memory_space_constraint(x, pltpu.HBM) for x in (tensor, factor_b.T, factor_c))
    small = pl.CostEstimate(flops=1_000_000, bytes_accessed=80_000, transcendentals=64)

    first = call(
        first_kernel,
        "first",
        [ANY, ANY],
        fast((racks, half, width), F32),
        [pltpu.VMEM(bt.shape, F32), pltpu.VMEM(factor_c.shape, F32), pltpu.SemaphoreType.DMA((2,))],
    )(bt, factor_c)
    first = lax.all_to_all(first, axes, 0, 0, tiled=True, axis_index_groups=gather_groups)
    other = lax.ppermute(first, "rows", [(r, r ^ 1) for r in range(lax.axis_size("rows"))])
    grams = call(grams_kernel, "grams", [VMEM] * 2, shape((rank, width), F32), cost_estimate=small)(first, other)
    arrived = lax.ppermute(grams, axes, pairs)
    mixed = call(
        mixed_kernel,
        "mixed",
        [ANY, VMEM, VMEM],
        fast((slabs, pods, half, width), F32),
        [pltpu.VMEM((SLOTS, ROWS, extent_k), F32), pltpu.SemaphoreType.DMA((SLOTS,))],
        cost_estimate=pl.CostEstimate(
            flops=4 * tensor.size * width, bytes_accessed=4 * tensor.size, transcendentals=0
        ),
    )(tensor, first, other)
    partial = call(partial_kernel, "partial", [VMEM] * 3, shape((racks * pods, width), F32))(mixed, first, other)
    grams = call(add_kernel, "add", [VMEM, VMEM, ANY], shape((rank, width), F32), cost_estimate=small)(
        grams, arrived, partial
    )
    parts = [grams] + [lax.ppermute(grams, "pods", [(p, p ^ n) for p in range(pods)]) for n in range(2, pods, 2)]
    everyone = lax.all_to_all(partial.reshape(racks * pods, 1, width), ("racks", "pods"), 0, 0, tiled=True)
    inverse = call(
        factor_kernel,
        "factor",
        [VMEM] * len(parts),
        shape((rank, 3 * rank), BF16),
        [pltpu.VMEM((len(parts), rank, width), F32), pltpu.VMEM((rank, rank), F32)],
        cost_estimate=small,
    )(*parts)
    return call(last_kernel, "last", [VMEM, VMEM], shape((slabs, rank), F32))(
        everyone.reshape(racks * pods, width), inverse
    )


def routes(mesh):
    rows, racks, pods = (mesh.shape[axis] for axis in ("rows", "racks", "pods"))

    def device(low, core, z, p):
        return ((low * 2 + core) * racks + z) * pods + p

    pairs = [
        (device(low, core, z, p), device(low ^ 1, core, z, p ^ 1))
        for low in range(rows // 2)
        for core in range(2)
        for z in range(racks)
        for p in range(pods)
    ]
    by_pods = [[device(low ^ (p % 2), 0, z, p) for p in range(pods)] for low in range(rows // 2) for z in range(racks)]
    by_racks = [[device(low, 1, z, p) for z in range(racks)] for low in range(rows // 2) for p in range(pods)]
    return pairs, by_pods + by_racks


def solution(mesh):
    pairs, groups = routes(mesh)

    def mapped(tensor, factor_b, factor_c):
        return body(pairs, groups, tensor, factor_b, factor_c)

    in_specs = (P("rows", "racks", "pods"), P(("racks", "pods"), None), P(("pods", "racks"), None))
    out_specs = P("rows", None)
    return jax.shard_map(mapped, mesh=mesh, in_specs=in_specs, out_specs=out_specs, check_vma=False)
```

```python
import jax
import jax.numpy as jnp
from jax import lax
from jax.experimental import pallas as pl
from jax.experimental.pallas import tpu as pltpu
from jax.sharding import PartitionSpec as P

F32, BF16 = jnp.float32, jnp.bfloat16
HIGHEST = lax.Precision.HIGHEST
VMEM = pl.BlockSpec(memory_space=pltpu.VMEM)
ANY = pl.BlockSpec(memory_space=pl.ANY)
LIMIT = 24 * 1024 * 1024
ROWS = 512


def pieces(x, n):
    out = []
    for _ in range(n - 1):
        out.append(x.astype(BF16))
        x = x - out[-1].astype(F32)
    return out + [x.astype(BF16)]


def product(x, y, dim):
    (a, b, c), (d, e, f) = pieces(x, 3), pieces(y, 3)
    left = jnp.concatenate([a, a, a, b, b, c], axis=dim)
    right = jnp.concatenate([d, e, f, d, e, d], axis=dim)
    return lax.dot_general(left, right, (((dim,), (dim,)), ((), ())), preferred_element_type=F32)


def fold(x, axis=0):
    half = x.shape[axis] // 2
    index = [slice(None)] * x.ndim
    upper, lower = list(index), list(index)
    upper[axis], lower[axis] = slice(0, half), slice(half, None)
    return jnp.concatenate([x[tuple(upper)], x[tuple(lower)]], axis=-1)


def unfold(x):
    rank = x.shape[-1] // 2
    return jnp.concatenate([x[..., :rank], x[..., rank:]], axis=-2)


def gathers_b():
    return lax.axis_index("rows") % 2 == 0


def first_kernel(bt_ref, c_ref, out_ref, bt, c, sems):
    copies = [
        pltpu.make_async_copy(source, to, sems.at[n]) for n, (source, to) in enumerate(((bt_ref, bt), (c_ref, c)))
    ]
    for copy in copies:
        copy.start()
    for copy in copies:
        copy.wait()
    rows = out_ref.shape[1]

    def send(block):
        for n in range(out_ref.shape[0]):
            out_ref[n, : block.shape[0]] = block

    @pl.when(gathers_b())
    def _():
        send(jnp.concatenate([bt[:, :rows].T, bt[:, rows:].T], axis=1))

    @pl.when(jnp.logical_not(gathers_b()))
    def _():
        grams = [fold(product(bt[...], bt[...], 1)), fold(product(c[...], c[...], 0))]
        block = jnp.concatenate([fold(c[...]), *grams], axis=0)
        send(jnp.concatenate([block, jnp.zeros((rows - block.shape[0], block.shape[1]), F32)], axis=0))


def grams_kernel(own_ref, other_ref, out_ref):
    rows = out_ref.shape[0]
    at = slice(rows // 2, rows // 2 + rows)
    out_ref[...] = jnp.sum(jnp.where(gathers_b(), other_ref[:, at], own_ref[:, at]), axis=0)


def add_kernel(x_ref, y_ref, after_ref, out_ref):
    out_ref[...] = x_ref[...] + y_ref[...]


def load_kernel(t_ref, after_ref, out_ref, sems):
    rows = out_ref.shape[1] // (sems.shape[0] // 2)
    copies = []
    for n in range(sems.shape[0]):
        i, j = n % 2, n // 2 * rows
        copies.append(
            pltpu.make_async_copy(t_ref.at[i, pl.ds(j, rows)], out_ref.at[i, pl.ds(j, rows)], sems.at[n])
        )
        copies[-1].start()
    for copy in copies:
        copy.wait()


def mixed_kernel(t_ref, own_ref, other_ref, out_ref):
    devices, _, width = own_ref.shape
    half = out_ref.shape[2]
    rank = width // 2
    slabs, extent_j, extent = t_ref.shape
    rows = extent // devices // 2
    c = jnp.where(gathers_b(), other_ref[:, :rows], own_ref[:, :rows])
    w = jnp.concatenate(pieces(unfold(c).reshape(extent, rank), 2), axis=1)
    left = lax.broadcasted_iota(jnp.int32, (half, width), 1) < rank
    for i in range(slabs):
        for n in range(0, extent_j, ROWS):
            high, low = pieces(t_ref[i, n : n + ROWS], 2)
            both = jnp.dot(high, w, preferred_element_type=F32) + jnp.dot(low, w, preferred_element_type=F32)
            both = both + pltpu.roll(both, rank, 1)
            for m in range(0, ROWS, 2 * half):
                part = both[m : m + 2 * half]
                out_ref[i, (n + m) // (2 * half)] = jnp.where(left, part[:half], part[half:])


def partial_kernel(mixed_ref, own_ref, other_ref, out_ref):
    half = mixed_ref.shape[2]
    width = mixed_ref.shape[3]
    mine = gathers_b()
    totals = [jnp.zeros((8, width), F32) for _ in range(2)]
    for n in range(mixed_ref.shape[1]):
        b = jnp.where(mine, own_ref[n], other_ref[n])
        for i in range(2):
            totals[i] = totals[i] + jnp.sum((mixed_ref[i, n] * b).reshape(half // 8, 8, width), axis=0)
    rows = []
    for total in totals:
        row = jnp.sum(total, axis=0, keepdims=True)
        rows.append(row + pltpu.roll(row, width // 2, 1))
    left = lax.broadcasted_iota(jnp.int32, (1, width), 1) < width // 2
    out_ref[...] = jnp.broadcast_to(jnp.where(left, rows[0], rows[1]), out_ref.shape)


def factor_kernel(*refs):
    parts, out_ref, (grams, inverse) = refs[:-3], refs[-3], refs[-2:]
    rank = inverse.shape[0]
    for n, part in enumerate(parts):
        grams[jnp.bitwise_xor(lax.axis_index("pods") // 2, n)] = part[...]
    both = grams[0]
    for n in range(1, len(parts)):
        both = both + grams[n]
    a = unfold(both[: rank // 2] * both[rank // 2 :])
    eye = lax.broadcasted_iota(jnp.int32, (rank, rank), 0) == lax.broadcasted_iota(jnp.int32, (rank, rank), 1)
    a = jnp.concatenate([a, eye.astype(F32)], axis=1)
    tile = 8
    tiles = [a[n : n + tile] for n in range(0, rank, tile)]

    def lanes(x, n):
        return jnp.broadcast_to(x[:, n : n + 1], x.shape)

    def sublanes(x, n):
        return jnp.broadcast_to(x[n : n + 1], x.shape)

    for t in range(len(tiles)):
        below = range(t, len(tiles))
        columns = {u: [lanes(tiles[u], tile * t + j) for j in range(tile)] for u in below}
        rows = [sublanes(tiles[t], j) for j in range(tile)]
        for j in range(tile):
            scale = lax.rsqrt(sublanes(columns[t][j], j))
            rows[j] = rows[j] * scale
            inverse[tile * t + j : tile * t + j + 1] = rows[j][:1, rank:]
            for u in below:
                columns[u][j] = columns[u][j] * scale
            for m in range(j + 1, tile):
                pivot = sublanes(columns[t][j], m)
                rows[m] = rows[m] - pivot * rows[j]
                for u in below:
                    columns[u][m] = columns[u][m] - columns[u][j] * pivot
        for u in below[1:]:
            for j in range(tile):
                tiles[u] = tiles[u] - columns[u][j] * rows[j]
    root = inverse[...]
    full = lax.dot_general(root, root, (((0,), (0,)), ((), ())), precision=HIGHEST, preferred_element_type=F32)
    out_ref[...] = jnp.concatenate(pieces(full, 3), axis=1)


def last_kernel(in_ref, inverse_ref, out_ref):
    rank = inverse_ref.shape[0]
    total = jnp.sum(in_ref[...], axis=0, keepdims=True)
    x = jnp.concatenate([total[:, :rank], total[:, rank:]], axis=0)
    parts = jnp.dot(jnp.concatenate(pieces(x, 3), axis=0), inverse_ref[...], preferred_element_type=F32)
    out_ref[...] = sum(
        parts[2 * n : 2 * n + 2, m * rank : (m + 1) * rank] for n in reversed(range(3)) for m in reversed(range(3 - n))
    )


def call(kernel, name, ins, outs, scratch=(), out=VMEM, **more):
    return pl.pallas_call(
        kernel,
        name=name,
        in_specs=ins,
        out_specs=out,
        out_shape=outs,
        scratch_shapes=scratch,
        compiler_params=pltpu.CompilerParams(vmem_limit_bytes=LIMIT),
        **more,
    )


def body(pairs, gather_groups, tensor, factor_b, factor_c):
    axes = ("rows", "racks", "pods")
    racks, pods = lax.axis_size("racks"), lax.axis_size("pods")
    slabs = tensor.shape[0]
    own_b, rank = factor_b.shape
    half, width = own_b // 2, 2 * rank
    shape, fast = jax.ShapeDtypeStruct, pltpu.VMEM
    tensor, bt, factor_c = (pltpu.with_memory_space_constraint(x, pltpu.HBM) for x in (tensor, factor_b.T, factor_c))
    small = pl.CostEstimate(flops=1_000_000, bytes_accessed=80_000, transcendentals=64)

    first = call(
        first_kernel,
        "first",
        [ANY, ANY],
        fast((racks, half, width), F32),
        [pltpu.VMEM(bt.shape, F32), pltpu.VMEM(factor_c.shape, F32), pltpu.SemaphoreType.DMA((2,))],
    )(bt, factor_c)
    first = lax.all_to_all(first, axes, 0, 0, tiled=True, axis_index_groups=gather_groups)
    other = lax.ppermute(first, "rows", [(r, r ^ 1) for r in range(lax.axis_size("rows"))])
    grams = call(grams_kernel, "grams", [VMEM] * 2, shape((rank, width), F32), cost_estimate=small)(first, other)
    arrived = lax.ppermute(grams, axes, pairs)
    loaded = call(
        load_kernel,
        "load",
        [ANY, ANY],
        fast(tensor.shape, F32),
        [pltpu.SemaphoreType.DMA((8,))],
        cost_estimate=pl.CostEstimate(flops=0, bytes_accessed=4 * tensor.size, transcendentals=0),
    )(tensor, first)
    mixed = call(
        mixed_kernel,
        "mixed",
        [VMEM] * 3,
        fast((slabs, pods, half, width), F32),
        cost_estimate=pl.CostEstimate(
            flops=4 * tensor.size * width, bytes_accessed=4 * tensor.size, transcendentals=0
        ),
    )(loaded, first, other)
    partial = call(partial_kernel, "partial", [VMEM] * 3, shape((racks * pods, width), F32))(mixed, first, other)
    grams = call(add_kernel, "add", [VMEM, VMEM, ANY], shape((rank, width), F32), cost_estimate=small)(
        grams, arrived, partial
    )
    parts = [grams] + [lax.ppermute(grams, "pods", [(p, p ^ n) for p in range(pods)]) for n in range(2, pods, 2)]
    everyone = lax.all_to_all(partial.reshape(racks * pods, 1, width), ("racks", "pods"), 0, 0, tiled=True)
    inverse = call(
        factor_kernel,
        "factor",
        [VMEM] * len(parts),
        shape((rank, 3 * rank), BF16),
        [pltpu.VMEM((len(parts), rank, width), F32), pltpu.VMEM((rank, rank), F32)],
        cost_estimate=small,
    )(*parts)
    return call(last_kernel, "last", [VMEM, VMEM], shape((slabs, rank), F32))(
        everyone.reshape(racks * pods, width), inverse
    )


def routes(mesh):
    rows, racks, pods = (mesh.shape[axis] for axis in ("rows", "racks", "pods"))

    def device(low, core, z, p):
        return ((low * 2 + core) * racks + z) * pods + p

    pairs = [
        (device(low, core, z, p), device(low ^ 1, core, z, p ^ 1))
        for low in range(rows // 2)
        for core in range(2)
        for z in range(racks)
        for p in range(pods)
    ]
    by_pods = [[device(low ^ (p % 2), 0, z, p) for p in range(pods)] for low in range(rows // 2) for z in range(racks)]
    by_racks = [[device(low, 1, z, p) for z in range(racks)] for low in range(rows // 2) for p in range(pods)]
    return pairs, by_pods + by_racks


def solution(mesh):
    pairs, groups = routes(mesh)

    def mapped(tensor, factor_b, factor_c):
        return body(pairs, groups, tensor, factor_b, factor_c)

    in_specs = (P("rows", "racks", "pods"), P(("racks", "pods"), None), P(("pods", "racks"), None))
    out_specs = P("rows", None)
    return jax.shard_map(mapped, mesh=mesh, in_specs=in_specs, out_specs=out_specs, check_vma=False)
```

```python
import jax
import jax.numpy as jnp
from jax import lax
from jax.experimental import pallas as pl
from jax.experimental.pallas import tpu as pltpu
from jax.sharding import PartitionSpec as P

F32, BF16 = jnp.float32, jnp.bfloat16
HIGHEST = lax.Precision.HIGHEST
VMEM = pl.BlockSpec(memory_space=pltpu.VMEM)
ANY = pl.BlockSpec(memory_space=pl.ANY)
LIMIT = 24 * 1024 * 1024
ROWS = 512


def pieces(x, n):
    out = []
    for _ in range(n - 1):
        out.append(x.astype(BF16))
        x = x - out[-1].astype(F32)
    return out + [x.astype(BF16)]


def product(x, y, dim):
    (a, b, c), (d, e, f) = pieces(x, 3), pieces(y, 3)
    left = jnp.concatenate([a, a, a, b, b, c], axis=dim)
    right = jnp.concatenate([d, e, f, d, e, d], axis=dim)
    return lax.dot_general(left, right, (((dim,), (dim,)), ((), ())), preferred_element_type=F32)


def fold(x, axis=0):
    half = x.shape[axis] // 2
    index = [slice(None)] * x.ndim
    upper, lower = list(index), list(index)
    upper[axis], lower[axis] = slice(0, half), slice(half, None)
    return jnp.concatenate([x[tuple(upper)], x[tuple(lower)]], axis=-1)


def unfold(x):
    rank = x.shape[-1] // 2
    return jnp.concatenate([x[..., :rank], x[..., rank:]], axis=-2)


def gathers_b():
    return lax.axis_index("rows") % 2 == 0


def first_kernel(bt_ref, c_ref, out_ref, bt, c, sems):
    copies = [
        pltpu.make_async_copy(source, to, sems.at[n]) for n, (source, to) in enumerate(((bt_ref, bt), (c_ref, c)))
    ]
    for copy in copies:
        copy.start()
    for copy in copies:
        copy.wait()
    rows = out_ref.shape[1]

    def send(block):
        for n in range(out_ref.shape[0]):
            out_ref[n, : block.shape[0]] = block

    @pl.when(gathers_b())
    def _():
        send(jnp.concatenate([bt[:, :rows].T, bt[:, rows:].T], axis=1))

    @pl.when(jnp.logical_not(gathers_b()))
    def _():
        grams = [fold(product(bt[...], bt[...], 1)), fold(product(c[...], c[...], 0))]
        block = jnp.concatenate([fold(c[...]), *grams], axis=0)
        send(jnp.concatenate([block, jnp.zeros((rows - block.shape[0], block.shape[1]), F32)], axis=0))


def grams_kernel(own_ref, other_ref, out_ref):
    rows = out_ref.shape[0]
    at = slice(rows // 2, rows // 2 + rows)
    out_ref[...] = jnp.sum(jnp.where(gathers_b(), other_ref[:, at], own_ref[:, at]), axis=0)


def add_kernel(x_ref, y_ref, after_ref, out_ref):
    out_ref[...] = x_ref[...] + y_ref[...]


def load_kernel(t_ref, after_ref, out_ref, sems):
    rows = out_ref.shape[1] // (sems.shape[0] // 2)
    copies = []
    for n in range(sems.shape[0]):
        i, j = n % 2, n // 2 * rows
        copies.append(
            pltpu.make_async_copy(t_ref.at[i, pl.ds(j, rows)], out_ref.at[i, pl.ds(j, rows)], sems.at[n])
        )
        copies[-1].start()
    for copy in copies:
        copy.wait()


def mixed_kernel(t_ref, own_ref, other_ref, out_ref):
    devices, _, width = own_ref.shape
    half = out_ref.shape[2]
    rank = width // 2
    slabs, extent_j, extent = t_ref.shape
    rows = extent // devices // 2
    c = jnp.where(gathers_b(), other_ref[:, :rows], own_ref[:, :rows])
    w = jnp.concatenate(pieces(unfold(c).reshape(extent, rank), 2), axis=1)
    left = lax.broadcasted_iota(jnp.int32, (half, width), 1) < rank
    for i in range(slabs):
        for n in range(0, extent_j, ROWS):
            high, low = pieces(t_ref[i, n : n + ROWS], 2)
            both = jnp.dot(high, w, preferred_element_type=F32) + jnp.dot(low, w, preferred_element_type=F32)
            both = both + pltpu.roll(both, rank, 1)
            for m in range(0, ROWS, 2 * half):
                part = both[m : m + 2 * half]
                out_ref[i, (n + m) // (2 * half)] = jnp.where(left, part[:half], part[half:])


def partial_kernel(mixed_ref, own_ref, other_ref, out_ref):
    half = mixed_ref.shape[2]
    width = mixed_ref.shape[3]
    mine = gathers_b()
    totals = [jnp.zeros((8, width), F32) for _ in range(2)]
    for n in range(mixed_ref.shape[1]):
        b = jnp.where(mine, own_ref[n], other_ref[n])
        for i in range(2):
            totals[i] = totals[i] + jnp.sum((mixed_ref[i, n] * b).reshape(half // 8, 8, width), axis=0)
    rows = []
    for total in totals:
        row = jnp.sum(total, axis=0, keepdims=True)
        rows.append(row + pltpu.roll(row, width // 2, 1))
    left = lax.broadcasted_iota(jnp.int32, (1, width), 1) < width // 2
    out_ref[...] = jnp.broadcast_to(jnp.where(left, rows[0], rows[1]), out_ref.shape)


def factor_kernel(*refs):
    parts, out_ref, (grams, inverse) = refs[:-3], refs[-3], refs[-2:]
    rank = inverse.shape[0]
    for n, part in zip((0, 2, 3, 1), parts, strict=True):
        grams[jnp.bitwise_xor(lax.axis_index("pods") // 2, n)] = part[...]
    both = grams[0]
    for n in range(1, len(parts)):
        both = both + grams[n]
    a = unfold(both[: rank // 2] * both[rank // 2 :])
    eye = lax.broadcasted_iota(jnp.int32, (rank, rank), 0) == lax.broadcasted_iota(jnp.int32, (rank, rank), 1)
    a = jnp.concatenate([a, eye.astype(F32)], axis=1)
    tile = 8
    tiles = [a[n : n + tile] for n in range(0, rank, tile)]

    def lanes(x, n):
        return jnp.broadcast_to(x[:, n : n + 1], x.shape)

    def sublanes(x, n):
        return jnp.broadcast_to(x[n : n + 1], x.shape)

    for t in range(len(tiles)):
        below = range(t, len(tiles))
        columns = {u: [lanes(tiles[u], tile * t + j) for j in range(tile)] for u in below}
        rows = [sublanes(tiles[t], j) for j in range(tile)]
        for j in range(tile):
            scale = lax.rsqrt(sublanes(columns[t][j], j))
            rows[j] = rows[j] * scale
            inverse[tile * t + j : tile * t + j + 1] = rows[j][:1, rank:]
            for u in below:
                columns[u][j] = columns[u][j] * scale
            for m in range(j + 1, tile):
                pivot = sublanes(columns[t][j], m)
                rows[m] = rows[m] - pivot * rows[j]
                for u in below:
                    columns[u][m] = columns[u][m] - columns[u][j] * pivot
        for u in below[1:]:
            for j in range(tile):
                tiles[u] = tiles[u] - columns[u][j] * rows[j]
    root = inverse[...]
    full = lax.dot_general(root, root, (((0,), (0,)), ((), ())), precision=HIGHEST, preferred_element_type=F32)
    out_ref[...] = jnp.concatenate(pieces(full, 3), axis=1)


def last_kernel(in_ref, inverse_ref, out_ref):
    rank = inverse_ref.shape[0]
    total = jnp.sum(in_ref[...], axis=0, keepdims=True)
    x = jnp.concatenate([total[:, :rank], total[:, rank:]], axis=0)
    parts = jnp.dot(jnp.concatenate(pieces(x, 3), axis=0), inverse_ref[...], preferred_element_type=F32)
    out_ref[...] = sum(
        parts[2 * n : 2 * n + 2, m * rank : (m + 1) * rank] for n in reversed(range(3)) for m in reversed(range(3 - n))
    )


def call(kernel, name, ins, outs, scratch=(), out=VMEM, **more):
    return pl.pallas_call(
        kernel,
        name=name,
        in_specs=ins,
        out_specs=out,
        out_shape=outs,
        scratch_shapes=scratch,
        compiler_params=pltpu.CompilerParams(vmem_limit_bytes=LIMIT),
        **more,
    )


def body(pairs, gather_groups, tensor, factor_b, factor_c):
    axes = ("rows", "racks", "pods")
    racks, pods = lax.axis_size("racks"), lax.axis_size("pods")
    slabs = tensor.shape[0]
    own_b, rank = factor_b.shape
    half, width = own_b // 2, 2 * rank
    shape, fast = jax.ShapeDtypeStruct, pltpu.VMEM
    tensor, bt, factor_c = (pltpu.with_memory_space_constraint(x, pltpu.HBM) for x in (tensor, factor_b.T, factor_c))
    small = pl.CostEstimate(flops=1_000_000, bytes_accessed=80_000, transcendentals=64)

    first = call(
        first_kernel,
        "first",
        [ANY, ANY],
        fast((racks, half, width), F32),
        [pltpu.VMEM(bt.shape, F32), pltpu.VMEM(factor_c.shape, F32), pltpu.SemaphoreType.DMA((2,))],
    )(bt, factor_c)
    first = lax.all_to_all(first, axes, 0, 0, tiled=True, axis_index_groups=gather_groups)
    other = lax.ppermute(first, "rows", [(r, r ^ 1) for r in range(lax.axis_size("rows"))])
    grams = call(grams_kernel, "grams", [VMEM] * 2, shape((rank, width), F32), cost_estimate=small)(first, other)
    arrived = lax.ppermute(grams, axes, pairs)
    loaded = call(
        load_kernel,
        "load",
        [ANY, ANY],
        fast(tensor.shape, F32),
        [pltpu.SemaphoreType.DMA((8,))],
        cost_estimate=pl.CostEstimate(flops=0, bytes_accessed=4 * tensor.size, transcendentals=0),
    )(tensor, first)
    mixed = call(
        mixed_kernel,
        "mixed",
        [VMEM] * 3,
        fast((slabs, pods, half, width), F32),
        cost_estimate=pl.CostEstimate(
            flops=4 * tensor.size * width, bytes_accessed=4 * tensor.size, transcendentals=0
        ),
    )(loaded, first, other)
    partial = call(partial_kernel, "partial", [VMEM] * 3, shape((racks * pods, width), F32))(mixed, first, other)
    grams = call(add_kernel, "add", [VMEM, VMEM, ANY], shape((rank, width), F32), cost_estimate=small)(
        grams, arrived, partial
    )
    order = (4, 6, 2)
    parts = [grams] + [lax.ppermute(grams, "pods", [(p, p ^ n) for p in range(pods)]) for n in order]
    everyone = lax.all_to_all(partial.reshape(racks * pods, 1, width), ("racks", "pods"), 0, 0, tiled=True)
    inverse = call(
        factor_kernel,
        "factor",
        [VMEM] * len(parts),
        shape((rank, 3 * rank), BF16),
        [pltpu.VMEM((len(parts), rank, width), F32), pltpu.VMEM((rank, rank), F32)],
        cost_estimate=small,
    )(*parts)
    return call(last_kernel, "last", [VMEM, VMEM], shape((slabs, rank), F32))(
        everyone.reshape(racks * pods, width), inverse
    )


def routes(mesh):
    rows, racks, pods = (mesh.shape[axis] for axis in ("rows", "racks", "pods"))

    def device(low, core, z, p):
        return ((low * 2 + core) * racks + z) * pods + p

    pairs = [
        (device(low, core, z, p), device(low ^ 1, core, z, p ^ 1))
        for low in range(rows // 2)
        for core in range(2)
        for z in range(racks)
        for p in range(pods)
    ]
    by_pods = [[device(low ^ (p % 2), 0, z, p) for p in range(pods)] for low in range(rows // 2) for z in range(racks)]
    by_racks = [[device(low, 1, z, p) for z in range(racks)] for low in range(rows // 2) for p in range(pods)]
    return pairs, by_pods + by_racks


def solution(mesh):
    pairs, groups = routes(mesh)

    def mapped(tensor, factor_b, factor_c):
        return body(pairs, groups, tensor, factor_b, factor_c)

    in_specs = (P("rows", "racks", "pods"), P(("racks", "pods"), None), P(("pods", "racks"), None))
    out_specs = P("rows", None)
    return jax.shard_map(mapped, mesh=mesh, in_specs=in_specs, out_specs=out_specs, check_vma=False)
```
